512 devices in a mesh: row: 32 (over y, x), col: 16 (over z, core).
Axes of the slice: x: 4, y: 8, z: 8, core: 2. Of those that a mesh axis runs over, the one named last changes fastest.
Arguments:
- tokens: bfloat16 [256, 8192], P('row', 'col'), may hold values from -6 to 6
- w_gate: bfloat16 [8192, 24576], P('col', 'row'), may hold values from -0.0625 to 0.0625
- w_up: bfloat16 [8192, 24576], P('col', 'row'), may hold values from -0.0625 to 0.0625
- w_down: bfloat16 [24576, 8192], P('row', 'col'), may hold values from -0.0390625 to 0.0390625
- target_table: bfloat16 [128, 8192], P(None, 'col'), may hold values from -6 to 6
- target_rows: int32 [128], P('row'), may hold values from 0 to 255, as said below
- buckets: int32 [128], P('row'), may hold values from 0 to 127
Outputs:
- output_y: bfloat16 [256, 8192], P('row', 'col')
- grad_tokens: bfloat16 [256, 8192], P('row', 'col')
- grad_gate: bfloat16 [8192, 24576], P('col', 'row')
- grad_up: bfloat16 [8192, 24576], P('col', 'row')
- grad_down: bfloat16 [24576, 8192], P('row', 'col')
The draws below stay inside these ranges and needn't reach their ends.
Inputs may be any that keep to these rules, and one draw needn't show every extreme that they name: `target_rows`: entries k * 4 to (k + 1) * 4 - 1 name distinct rows among rows k * 8 to (k + 1) * 8 - 1.
All inputs are finite; a program needn't handle non-finite values.
Results may differ from the reference program's by a relative error of at most 0.008.
Values may be sent and summed in bfloat16 or wider, within the bound.
A program may use at most 64 MiB of HBM per device.

```python
import jax
import jax.numpy as jnp

D = 8192
FF = 24576
BUCKETS = 128
TOK_ROW = 8
TGT_ROW = 4
TOKENS = 256
TARGETS = 128


def draw_target_rows(key, part):
    key = jax.random.fold_in(key, 11)
    groups = TOKENS // TOK_ROW
    scores = jax.random.randint(key, (groups, TOK_ROW), 0, 1 << 20, dtype=jnp.int32)
    scores = scores * TOK_ROW + jnp.arange(TOK_ROW, dtype=jnp.int32)[None, :]
    order = jnp.argsort(scores, axis=1, stable=True)[:, :TGT_ROW].astype(jnp.int32)
    offsets = (jnp.arange(groups, dtype=jnp.int32) * TOK_ROW)[:, None]
    return (order + offsets).reshape(-1).astype(jnp.int32)


def plant(array, own_key, smallest, largest):
    shape = array.shape
    spot = [jax.random.randint(jax.random.fold_in(own_key, axis), (), 0, shape[axis]) for axis in range(len(shape))]
    array = array.at[tuple(spot)].set(smallest)
    longest = shape.index(max(shape))
    spot[longest] = (spot[longest] + 1) % shape[longest]
    return array.at[tuple(spot)].set(largest)


def block_scale(key, shape, pieces, least, high):
    factor_of = 1.0
    for dim, shards_of in pieces:
        heights = jax.random.uniform(jax.random.fold_in(jax.random.fold_in(key, 6), dim), (shards_of,), jnp.float32, least / len(pieces), high / len(pieces))
        factor_of = factor_of * jnp.repeat(jnp.exp(heights), shape[dim] // shards_of).reshape((-1,) + (1,) * (len(shape) - 1 - dim))
    return factor_of


def normal_values(stream_key, dims, width, bound, cuts=(), kind=jnp.bfloat16):
    array = width * jax.random.normal(stream_key, dims, jnp.float32)
    if cuts:
        array = array * block_scale(stream_key, dims, cuts, -0.22, 0.18)
    return jnp.clip(array, -bound, bound).astype(kind)


def setup_inputs(seed: int = 0) -> dict:
    key_of = jax.random.split(jax.random.key(seed), 8)
    return {
        "tokens": normal_values(key_of[0], (TOKENS, D), 1.0, 6.0, ((0, 32), (1, 16))),
        "w_gate": normal_values(key_of[1], (D, FF), D ** -0.5, 0.0625, ((0, 16), (1, 32))),
        "w_up": normal_values(key_of[2], (D, FF), D ** -0.5, 0.0625, ((0, 16), (1, 32))),
        "w_down": normal_values(key_of[3], (FF, D), FF ** -0.5, 0.0390625, ((0, 32), (1, 16))),
        "target_table": normal_values(key_of[4], (BUCKETS, D), 1.0, 6.0, ((1, 16),)),
        "target_rows": draw_target_rows(jax.random.fold_in(key_of[7], 71), 0),
        "buckets": plant(jax.random.randint(key_of[6], (TARGETS,), 0, BUCKETS), jax.random.fold_in(key_of[6], 1), 0, BUCKETS - 1).astype(jnp.int32),
    }


def reference(tokens, w_gate, w_up, w_down, target_table, target_rows, buckets):
    gate = jnp.dot(tokens, w_gate, preferred_element_type=jnp.float32)
    up = jnp.dot(tokens, w_up, preferred_element_type=jnp.float32)
    sig = jax.nn.sigmoid(gate)
    hidden = (gate * sig * up).astype(jnp.bfloat16)
    output_y = jnp.dot(hidden, w_down, preferred_element_type=jnp.float32).astype(jnp.bfloat16)
    onehot = (buckets[:, None] == jnp.arange(BUCKETS, dtype=jnp.int32)[None, :]).astype(jnp.bfloat16)
    targets = jnp.dot(onehot, target_table, preferred_element_type=jnp.float32)
    diff = 0.25 * (output_y[target_rows].astype(jnp.float32) - targets)
    grad_y = jnp.zeros((TOKENS, D), jnp.float32).at[target_rows].set(diff).astype(jnp.bfloat16)
    grad_down = jnp.dot(hidden.T, grad_y, preferred_element_type=jnp.float32).astype(jnp.bfloat16)
    grad_hidden = jnp.dot(grad_y, w_down.T, preferred_element_type=jnp.float32)
    gate_act = (grad_hidden * up * sig * (1.0 + gate * (1.0 - sig))).astype(jnp.bfloat16)
    up_act = (grad_hidden * gate * sig).astype(jnp.bfloat16)
    grad_gate = jnp.dot(tokens.T, gate_act, preferred_element_type=jnp.float32).astype(jnp.bfloat16)
    grad_up = jnp.dot(tokens.T, up_act, preferred_element_type=jnp.float32).astype(jnp.bfloat16)
    first = jnp.dot(gate_act, w_gate.T, preferred_element_type=jnp.float32)
    grad_tokens = (first + jnp.dot(up_act, w_up.T, preferred_element_type=jnp.float32)).astype(jnp.bfloat16)
    return output_y, grad_tokens, grad_gate, grad_up, grad_down
```

```python
import jax
import jax.numpy as jnp
from jax import lax
from jax.experimental import pallas as pl
from jax.experimental.pallas import tpu as pltpu
from jax.sharding import PartitionSpec as P

MESH = pl.DeviceIdType.MESH
BF16, F32 = jnp.bfloat16, jnp.float32

NY, NX, NZ = 8, 4, 8
ROWS = NY * NX
HALF = 4
LANES = 128
TOK = ROWS * HALF

(
    S_A0, S_A1, S_BP0, S_BP1, S_B0, S_B1, S_C0, S_C1, S_CP0, S_CP1, S_D0, S_D1,
    S_E, S_FP, S_F, S_G, S_GP, S_H, NUM_SEMS,
) = range(19)


def zigzag(m, n):
    half = (m + 1) // 2
    return n // 2 + jnp.where(m % 2 == 0, half, -half)


def dot(left, right, dims):
    return lax.dot_general(left, right, ((dims[0], dims[1]), ((), ())), preferred_element_type=F32)


def kernel(
    rows_s, buckets_s, tokens_ref, wg_hbm, wu_hbm, wd_hbm, table_hbm,
    y_out, gt_out, gg_out, gu_out, gd_out,
    wg, wu, wd, table,
    xs, xr, f_in, x_mat,
    gu_part, gu_psend, gu_precv, gu_zsend, gu_zrecv, gu_keep,
    hc, h_mat,
    f_out, y_send, y_recv, y_keep, tgt,
    gy_send, gy_recv, gy_mat,
    gh_part, gh_psend, gh_precv, gh_zsend, gh_zrecv,
    ac, act_mat, gt_send, gt_recv,
    send_sem, recv_sem, load_sem,
):
    row, col = lax.axis_index("row"), lax.axis_index("col")
    y, x, z, k = row // NX, row % NX, col // 2, col % 2
    width = wg.shape[1]
    wide = wg.shape[0]
    chunks = wide // LANES
    half_width = width // 2

    loads = [
        pltpu.make_async_copy(src, dst, load_sem.at[i])
        for i, (src, dst) in enumerate([(wg_hbm, wg), (wu_hbm, wu), (wd_hbm, wd), (table_hbm, table)])
    ]
    for load in loads:
        load.start()

    def row_peer(m, sign):
        dy, dx = zigzag(m // NX, NY), zigzag(m % NX, NX)
        return (((y + NY + sign * dy) % NY) * NX + (x + NX + sign * dx) % NX, col)

    def z_peer(m):
        return (z + zigzag(m, NZ)) % NZ

    partner = (row, z * 2 + 1 - k)

    barrier = pltpu.get_barrier_semaphore()

    def greet_row(m, carry):
        pl.semaphore_signal(barrier, inc=1, device_id=row_peer(m, 1), device_id_type=MESH)
        return carry

    def greet_col(m, carry):
        pl.semaphore_signal(barrier, inc=1, device_id=(row, z_peer(m) * 2 + k), device_id_type=MESH)
        return carry

    lax.fori_loop(0, ROWS - 1, greet_row, 0)
    lax.fori_loop(0, NZ - 1, greet_col, 0)
    pl.semaphore_signal(barrier, inc=1, device_id=partner, device_id_type=MESH)

    tgt_pos = [rows_s[i] - 2 * HALF * row for i in range(HALF)]
    rest_pos = [jnp.int32(0)] * HALF
    seen = jnp.int32(0)
    for t in range(2 * HALF):
        is_target = jnp.int32(0)
        for p in tgt_pos:
            is_target = is_target + jnp.where(p == t, 1, 0)
        for i in range(HALF):
            rest_pos[i] = rest_pos[i] + jnp.where(seen == i, 1 - is_target, 0) * t
        seen = seen + 1 - is_target
    pos = [tgt_pos, rest_pos]

    tok = tokens_ref[...].astype(F32)
    iota8 = lax.broadcasted_iota(jnp.int32, tok.shape, 0)
    iota16 = lax.broadcasted_iota(jnp.int32, (16, LANES), 0)
    for h in range(2):
        packed = jnp.zeros((16, LANES), F32)
        for i in range(HALF):
            line = jnp.sum(jnp.where(iota8 == pos[h][i], tok, 0.0), axis=0, keepdims=True)
            for j in range(chunks):
                piece = line[:, j * LANES : (j + 1) * LANES]
                packed = jnp.where(iota16 == j * HALF + i, piece, packed)
        xs[h] = packed.astype(BF16)
        xr[h, ROWS - 1] = packed.astype(BF16)

    loads[3].wait()
    targets = jnp.zeros((16, LANES), F32)
    lane16 = lax.broadcasted_iota(jnp.int32, (16, table.shape[0]), 1)
    sub16 = lax.broadcasted_iota(jnp.int32, (16, table.shape[0]), 0)
    for j in range(chunks):
        onehot = jnp.zeros((16, table.shape[0]), F32)
        for i in range(HALF):
            hit = jnp.logical_and(sub16 == j * HALF + i, lane16 == buckets_s[i])
            onehot = jnp.where(hit, 1.0, onehot)
        targets = targets + dot(onehot.astype(BF16), table[:, j * LANES : (j + 1) * LANES], ((1,), (0,)))
    tgt[...] = targets

    pl.semaphore_wait(barrier, ROWS - 1 + NZ - 1 + 1)

    def wait_recv(ref, s):
        pltpu.make_async_copy(ref, ref, recv_sem.at[s]).wait()

    def wait_send(ref, s):
        pltpu.make_async_copy(ref, ref, send_sem.at[s]).wait()

    def remote(src, dst, s, device):
        pltpu.make_async_remote_copy(
            src_ref=src, dst_ref=dst, send_sem=send_sem.at[s], recv_sem=recv_sem.at[s],
            device_id=device, device_id_type=MESH,
        ).start()

    def spread_rows(src, dst, s):
        def one(m, carry):
            remote(src, dst.at[m], s, row_peer(m, 1))
            return carry

        lax.fori_loop(0, ROWS - 1, one, 0)

    def scatter_rows(src, dst, s):
        def one(m, carry):
            remote(src.at[m], dst.at[m], s, row_peer(m, -1))
            return carry

        lax.fori_loop(0, ROWS - 1, one, 0)

    def scatter_z(src, dst, s):
        def one(m, carry):
            peer = z_peer(m)
            remote(src.at[peer], dst.at[z], s, (row, peer * 2 + k))
            return carry

        lax.fori_loop(0, NZ - 1, one, 0)

    def spread_z(buf, s):
        def one(m, carry):
            remote(buf.at[k, z], buf.at[k, z], s, (row, z_peer(m) * 2 + k))
            return carry

        lax.fori_loop(0, NZ - 1, one, 0)

    def others(buf, n):
        return buf.at[pl.ds(0, n - 1)]

    def to_matrix(buf, out):
        f_in[...] = buf[...].astype(F32).reshape(ROWS * 16, LANES)
        for j in range(chunks):
            parts = [f_in[pl.ds(j * HALF + i, ROWS, stride=16), :] for i in range(HALF)]
            out[:, j * LANES : (j + 1) * LANES] = jnp.concatenate(parts, axis=0).astype(BF16)

    def from_matrix(mat, out):
        for j in range(chunks):
            for i in range(HALF):
                f_out[pl.ds(j * HALF + i, ROWS, stride=16), :] = mat[
                    i * ROWS : (i + 1) * ROWS, j * LANES : (j + 1) * LANES
                ]
        out[...] = f_out[...].reshape(ROWS, 16, LANES).astype(BF16)

    def row_total(recv):
        own = f_out[(ROWS - 1) * 16 : ROWS * 16, :]
        return own + jnp.sum(recv[...].astype(F32), axis=0)

    def unpack(first, second, out):
        iota = lax.broadcasted_iota(jnp.int32, (2 * HALF, LANES), 0)
        for j in range(chunks):
            block = jnp.zeros((2 * HALF, LANES), F32)
            for h, v in enumerate((first, second)):
                for i in range(HALF):
                    at = j * HALF + i
                    block = jnp.where(iota == pos[h][i], v[at : at + 1, :], block)
            out[:, j * LANES : (j + 1) * LANES] = block.astype(BF16)

    def gate_up_part(h):
        to_matrix(xr.at[h], x_mat.at[h])
        xm = x_mat[h]
        gate = dot(xm, wg[...], ((1,), (0,)))
        gu_part[:, :, 0:8, :] = gate.reshape(2, NZ, 8, width)
        up = dot(xm, wu[...], ((1,), (0,)))
        gu_part[:, :, 8:16, :] = up.reshape(2, NZ, 8, width)
        gu_psend[h] = gu_part[1 - k].astype(BF16)
        remote(gu_psend.at[h], gu_precv.at[h], S_BP0 + h, partner)

    def gate_up_scatter(h):
        wait_recv(gu_precv.at[h], S_BP0 + h)
        gu_zsend[h] = (gu_part[k] + gu_precv[h].astype(F32)).astype(BF16)
        gu_zrecv[h, z] = gu_zsend[h, z]
        scatter_z(gu_zsend.at[h], gu_zrecv.at[h], S_B0 + h)

    def hidden_spread(h):
        wait_recv(others(gu_zrecv.at[h], NZ), S_B0 + h)
        both = jnp.sum(gu_zrecv[h].astype(F32), axis=0)
        if h == 0:
            gu_keep[...] = both
        gate, up = both[0:8], both[8:16]
        hid = gate * jax.nn.sigmoid(gate) * up
        hc[h, k, z] = jnp.concatenate([hid[:, :half_width], hid[:, half_width:]], axis=0).astype(BF16)
        spread_z(hc.at[h], S_C0 + h)

    def hidden_pair(h):
        wait_recv(others(hc.at[h, 0], NZ), S_C0 + h)
        remote(hc.at[h, k], hc.at[h, k], S_CP0 + h, partner)

    def output_scatter(h):
        wait_recv(hc.at[h, 0], S_CP0 + h)
        v = hc[h].astype(F32).reshape(2 * NZ, 16, half_width)
        h_mat[h, :, :half_width] = v[:, 0:8].reshape(TOK, half_width).astype(BF16)
        h_mat[h, :, half_width:] = v[:, 8:16].reshape(TOK, half_width).astype(BF16)
        from_matrix(dot(h_mat[h], wd[...], ((1,), (0,))), y_send.at[h])
        y_keep[h] = f_out[(ROWS - 1) * 16 : ROWS * 16, :]
        scatter_rows(y_send.at[h], y_recv.at[h], S_D0 + h)

    def output_total(h):
        wait_recv(y_recv.at[h], S_D0 + h)
        total = y_keep[h] + jnp.sum(y_recv[h].astype(F32), axis=0)
        y_keep[h] = total.astype(BF16).astype(F32)

    spread_rows(xs.at[0], xr.at[0], S_A0)
    loads[0].wait()
    loads[1].wait()
    loads[2].wait()
    wait_recv(others(xr.at[0], ROWS), S_A0)
    gate_up_part(0)
    gate_up_scatter(0)
    spread_rows(xs.at[1], xr.at[1], S_A1)
    hidden_spread(0)
    wait_recv(others(xr.at[1], ROWS), S_A1)
    gate_up_part(1)
    hidden_pair(0)
    output_scatter(0)
    gate_up_scatter(1)
    output_total(0)

    gy = (0.25 * (y_keep[0] - tgt[...])).astype(BF16)
    gy_send[...] = gy
    gy_recv[ROWS - 1] = gy
    spread_rows(gy_send, gy_recv, S_E)
    hidden_spread(1)
    wait_recv(others(gy_recv, ROWS), S_E)

    to_matrix(gy_recv, gy_mat)
    gh = dot(gy_mat[...], wd[...], ((1,), (1,))).reshape(2, NZ, 8, width)
    gh_part[:, :, 0:8, :] = gh[:, :, :, :half_width]
    gh_part[:, :, 8:16, :] = gh[:, :, :, half_width:]
    gh_psend[...] = gh_part[1 - k].astype(BF16)
    remote(gh_psend, gh_precv, S_FP, partner)
    wait_recv(gh_precv, S_FP)
    gh_zsend[...] = (gh_part[k] + gh_precv[...].astype(F32)).astype(BF16)
    gh_zrecv[z] = gh_zsend[z]
    scatter_z(gh_zsend, gh_zrecv, S_F)
    hidden_pair(1)
    output_scatter(1)
    wait_recv(others(gh_zrecv, NZ), S_F)
    total = jnp.sum(gh_zrecv[...].astype(F32), axis=0)
    grad_hidden = jnp.concatenate([total[0:8], total[8:16]], axis=1)
    gate, up = gu_keep[0:8], gu_keep[8:16]
    sig = jax.nn.sigmoid(gate)
    gate_act = grad_hidden * up * sig * (1.0 + gate * (1.0 - sig))
    up_act = grad_hidden * gate * sig
    ac[k, z] = jnp.concatenate([gate_act, up_act], axis=0).astype(BF16)
    spread_z(ac, S_G)
    gd_out[...] = dot(h_mat[0], gy_mat[...], ((0,), (0,))).astype(BF16)
    wait_recv(others(ac.at[0], NZ), S_G)
    remote(ac.at[k], ac.at[k], S_GP, partner)
    wait_recv(ac.at[0], S_GP)
    v = ac[...].astype(F32).reshape(2 * NZ, 16, width)
    act_mat[0] = v[:, 0:8].reshape(TOK, width).astype(BF16)
    act_mat[1] = v[:, 8:16].reshape(TOK, width).astype(BF16)
    grad = dot(act_mat[0], wg[...], ((1,), (1,))) + dot(act_mat[1], wu[...], ((1,), (1,)))
    from_matrix(grad, gt_send)
    scatter_rows(gt_send, gt_recv, S_H)
    output_total(1)
    unpack(y_keep[0], y_keep[1], y_out)
    gg_out[...] = dot(x_mat[0], act_mat[0], ((0,), (0,))).astype(BF16)
    gu_out[...] = dot(x_mat[0], act_mat[1], ((0,), (0,))).astype(BF16)
    wait_recv(gt_recv, S_H)
    unpack(row_total(gt_recv), jnp.zeros((16, LANES), F32), gt_out)

    for h in range(2):
        wait_send(others(xr.at[h], ROWS), S_A0 + h)
        wait_send(gu_precv.at[h], S_BP0 + h)
        wait_send(others(gu_zrecv.at[h], NZ), S_B0 + h)
        wait_send(others(hc.at[h, 0], NZ), S_C0 + h)
        wait_send(hc.at[h, 0], S_CP0 + h)
        wait_send(y_recv.at[h], S_D0 + h)
    wait_send(others(gy_recv, ROWS), S_E)
    wait_send(gh_precv, S_FP)
    wait_send(others(gh_zrecv, NZ), S_F)
    wait_send(others(ac.at[0], NZ), S_G)
    wait_send(ac.at[0], S_GP)
    wait_send(gt_recv, S_H)


def on_device(tokens, w_gate, w_up, w_down, target_table, target_rows, buckets):
    wide, width = w_gate.shape
    half_width = width // 2
    vmem, smem, anywhere = (pl.BlockSpec(memory_space=s) for s in (pltpu.VMEM, pltpu.SMEM, pl.ANY))
    outs = (tokens, tokens, w_gate, w_up, w_down)
    return pl.pallas_call(
        kernel,
        out_shape=tuple(jax.ShapeDtypeStruct(a.shape, BF16) for a in outs),
        in_specs=[smem, smem, vmem, anywhere, anywhere, anywhere, anywhere],
        out_specs=(vmem,) * 5,
        scratch_shapes=[
            pltpu.VMEM(w_gate.shape, BF16),
            pltpu.VMEM(w_up.shape, BF16),
            pltpu.VMEM(w_down.shape, BF16),
            pltpu.VMEM(target_table.shape, BF16),
            pltpu.VMEM((2, 16, LANES), BF16),
            pltpu.VMEM((2, ROWS, 16, LANES), BF16),
            pltpu.VMEM((ROWS * 16, LANES), F32),
            pltpu.VMEM((2, TOK, wide), BF16),
            pltpu.VMEM((2, NZ, 16, width), F32),
            pltpu.VMEM((2, NZ, 16, width), BF16),
            pltpu.VMEM((2, NZ, 16, width), BF16),
            pltpu.VMEM((2, NZ, 16, width), BF16),
            pltpu.VMEM((2, NZ, 16, width), BF16),
            pltpu.VMEM((16, width), F32),
            pltpu.VMEM((2, 2, NZ, 16, half_width), BF16),
            pltpu.VMEM((2, TOK, width), BF16),
            pltpu.VMEM((ROWS * 16, LANES), F32),
            pltpu.VMEM((2, ROWS, 16, LANES), BF16),
            pltpu.VMEM((2, ROWS - 1, 16, LANES), BF16),
            pltpu.VMEM((2, 16, LANES), F32),
            pltpu.VMEM((16, LANES), F32),
            pltpu.VMEM((16, LANES), BF16),
            pltpu.VMEM((ROWS, 16, LANES), BF16),
            pltpu.VMEM((TOK, wide), BF16),
            pltpu.VMEM((2, NZ, 16, half_width), F32),
            pltpu.VMEM((NZ, 16, half_width), BF16),
            pltpu.VMEM((NZ, 16, half_width), BF16),
            pltpu.VMEM((NZ, 16, half_width), BF16),
            pltpu.VMEM((NZ, 16, half_width), BF16),
            pltpu.VMEM((2, NZ, 16, width), BF16),
            pltpu.VMEM((2, TOK, width), BF16),
            pltpu.VMEM((ROWS, 16, LANES), BF16),
            pltpu.VMEM((ROWS - 1, 16, LANES), BF16),
            pltpu.SemaphoreType.DMA((NUM_SEMS,)),
            pltpu.SemaphoreType.DMA((NUM_SEMS,)),
            pltpu.SemaphoreType.DMA((4,)),
        ],
        compiler_params=pltpu.CompilerParams(
            collective_id=0, has_side_effects=True, vmem_limit_bytes=48 * 1024 * 1024
        ),
        name="swiglu_step",
    )(target_rows, buckets, tokens, w_gate, w_up, w_down, target_table)


def solution(mesh):
    in_specs = (
        P("row", "col"),
        P("col", "row"),
        P("col", "row"),
        P("row", "col"),
        P(None, "col"),
        P("row"),
        P("row"),
    )
    out_specs = (
        P("row", "col"),
        P("row", "col"),
        P("col", "row"),
        P("col", "row"),
        P("row", "col"),
    )
    return jax.shard_map(
        on_device, mesh=mesh, in_specs=in_specs, out_specs=out_specs, check_vma=False
    )
```

```python
import jax
import jax.numpy as jnp
from jax import lax
from jax.experimental import pallas as pl
from jax.experimental.pallas import tpu as pltpu
from jax.sharding import PartitionSpec as P

VMEM_BYTES = 60 * 1024 * 1024
PIECES = 4
MESH = pl.DeviceIdType.MESH
BF16, F32 = jnp.bfloat16, jnp.float32

NY, NX, NZ = 8, 4, 8
ROWS = NY * NX
HALF = 4
LANES = 128
TOK = ROWS * HALF

(
    S_A0, S_A1, S_BP0, S_BP1, S_B0, S_B1, S_C0, S_C1, S_CP, S_D0, S_D1,
    S_E, S_EP, S_F, S_G, S_GP, S_H, S_WD, S_TG, S_Y, NUM_SEMS,
) = range(21)
PAIR = HALF // 2


def zigzag(m, n):
    half = (m + 1) // 2
    return n // 2 + jnp.where(m % 2 == 0, half, -half)


def dot(left, right, dims):
    return lax.dot_general(left, right, ((dims[0], dims[1]), ((), ())), preferred_element_type=F32)


def kernel(
    rows_hbm, buckets_hbm, tokens_hbm, wg_hbm, wu_hbm, wd_hbm, table_hbm,
    y_hbm, gt_hbm, gg_hbm, gu_hbm, gd_hbm,
    rows_s, buckets_s, tokens_ref, table, wg, wu, wd,
    xs, xr, f_in, x_mat,
    gu_part, gu_psend, gu_precv, gu_zsend, gu_zrecv, gu_keep,
    hc, h_mat,
    f_out, y_send, y_recv, y_keep, y_give, y_take, tgt, tgt_give,
    gy_send, gy_recv, gy_mat, gy_give,
    gh_zsend, gh_zrecv,
    ac, act_mat, gt_send, gt_recv,
    y_out, gt_out, gg_out, gu_out, gd_out,
    send_sem, recv_sem, load_sem, store_sem, pair_sem, act_sem,
):
    row, col = lax.axis_index("row"), lax.axis_index("col")
    y, x, z, k = row // NX, row % NX, col // 2, col % 2
    width = wg.shape[1]
    wide = wg.shape[0]
    chunks = wide // LANES
    half_width = width // 2

    loads = [
        pltpu.make_async_copy(src, dst, load_sem.at[i])
        for i, (src, dst) in enumerate(
            [
                (rows_hbm, rows_s), (buckets_hbm, buckets_s), (tokens_hbm, tokens_ref), (table_hbm, table),
                (wg_hbm, wg), (wu_hbm, wu), (wd_hbm, wd.at[k]),
            ]
        )
    ]
    for load in loads:
        load.start()

    stores = [
        pltpu.make_async_copy(src, dst, store_sem.at[i])
        for i, (src, dst) in enumerate(
            [(y_out, y_hbm), (gt_out, gt_hbm), (gg_out, gg_hbm), (gu_out, gu_hbm), (gd_out, gd_hbm)]
        )
    ]

    def row_peer(m, sign):
        dy, dx = zigzag(m // NX, NY), zigzag(m % NX, NX)
        return (((y + NY + sign * dy) % NY) * NX + (x + NX + sign * dx) % NX, col)

    def z_peer(m):
        return (z + zigzag(m, NZ)) % NZ

    partner = (row, z * 2 + 1 - k)

    barrier = pltpu.get_barrier_semaphore()

    def greet_row(m, carry):
        pl.semaphore_signal(barrier, inc=1, device_id=row_peer(m, 1), device_id_type=MESH)
        return carry

    def greet_col(m, carry):
        pl.semaphore_signal(barrier, inc=1, device_id=(row, z_peer(m) * 2 + k), device_id_type=MESH)
        return carry

    lax.fori_loop(0, ROWS - 1, greet_row, 0)
    lax.fori_loop(0, NZ - 1, greet_col, 0)
    pl.semaphore_signal(barrier, inc=1, device_id=partner, device_id_type=MESH)

    loads[0].wait()
    loads[2].wait()
    tgt_pos = [rows_s[i] - 2 * HALF * row for i in range(HALF)]
    rest_pos = [jnp.int32(0)] * HALF
    seen = jnp.int32(0)
    for t in range(2 * HALF):
        is_target = jnp.int32(0)
        for p in tgt_pos:
            is_target = is_target + jnp.where(p == t, 1, 0)
        for i in range(HALF):
            rest_pos[i] = rest_pos[i] + jnp.where(seen == i, 1 - is_target, 0) * t
        seen = seen + 1 - is_target
    pos = [tgt_pos, rest_pos]

    tok = tokens_ref[...].astype(F32)
    iota8 = lax.broadcasted_iota(jnp.int32, tok.shape, 0)
    iota16 = lax.broadcasted_iota(jnp.int32, (16, LANES), 0)
    for h in range(2):
        packed = jnp.zeros((16, LANES), F32)
        for i in range(HALF):
            line = jnp.sum(jnp.where(iota8 == pos[h][i], tok, 0.0), axis=0, keepdims=True)
            for j in range(chunks):
                piece = line[:, j * LANES : (j + 1) * LANES]
                packed = jnp.where(iota16 == j * HALF + i, piece, packed)
        xs[h] = packed.astype(BF16)
        xr[h, ROWS - 1] = packed.astype(BF16)

    loads[1].wait()
    loads[3].wait()
    targets = jnp.zeros((16, LANES), F32)
    lane16 = lax.broadcasted_iota(jnp.int32, (16, table.shape[0]), 1)
    sub16 = lax.broadcasted_iota(jnp.int32, (16, table.shape[0]), 0)
    for j in range(chunks):
        onehot = jnp.zeros((16, table.shape[0]), F32)
        for i in range(HALF):
            at = i // PAIR * 8 + j * PAIR + i % PAIR
            hit = jnp.logical_and(sub16 == at, lane16 == buckets_s[i])
            onehot = jnp.where(hit, 1.0, onehot)
        targets = targets + dot(onehot.astype(BF16), table[:, j * LANES : (j + 1) * LANES], ((1,), (0,)))
    first = (jnp.zeros((8, LANES), jnp.int32) + k) == 0
    tgt[k] = jnp.where(first, targets[0:8], targets[8:16])
    tgt_give[...] = jnp.where(first, targets[8:16], targets[0:8])

    pl.semaphore_wait(barrier, ROWS - 1 + NZ - 1 + 1)

    def wait_recv(ref, s):
        pltpu.make_async_copy(ref, ref, recv_sem.at[s]).wait()

    def wait_send(ref, s):
        pltpu.make_async_copy(ref, ref, send_sem.at[s]).wait()

    def remote(src, dst, s, device, arrived=None):
        pltpu.make_async_remote_copy(
            src_ref=src, dst_ref=dst, send_sem=send_sem.at[s],
            recv_sem=recv_sem.at[s] if arrived is None else arrived,
            device_id=device, device_id_type=MESH,
        ).start()

    def spread_rows(src, dst, s):
        def one(m, carry):
            remote(src, dst.at[m], s, row_peer(m, 1))
            return carry

        lax.fori_loop(0, ROWS - 1, one, 0)

    def scatter_rows(src, dst, s):
        def one(m, carry):
            remote(src.at[m], dst.at[m], s, row_peer(m, -1))
            return carry

        lax.fori_loop(0, ROWS - 1, one, 0)

    def scatter_z(src, dst, s):
        def one(m, carry):
            peer = z_peer(m)
            remote(src.at[peer], dst.at[z], s, (row, peer * 2 + k))
            return carry

        lax.fori_loop(0, NZ - 1, one, 0)

    def spread_z(buf, s, arrived=None):
        def one(m, carry):
            here = buf.at[k, z]
            remote(here, here, s, (row, z_peer(m) * 2 + k), None if arrived is None else arrived.at[m])
            return carry

        lax.fori_loop(0, NZ - 1, one, 0)

    def others(buf, n):
        return buf.at[pl.ds(0, n - 1)]

    def load_rows(buf):
        f_in[...] = buf[...].astype(F32).reshape(ROWS * 16, LANES)

    def columns(at, tokens):
        parts = [f_in[pl.ds(at + i, ROWS, stride=16), :] for i in range(tokens)]
        return jnp.concatenate(parts, axis=0).astype(BF16)

    def put_columns(mat, at, tokens):
        for i in range(tokens):
            f_out[pl.ds(at + i, ROWS, stride=16), :] = mat[i * ROWS : (i + 1) * ROWS]

    def store_rows(out):
        out[...] = f_out[...].reshape(ROWS, 16, LANES).astype(BF16)

    def part(j):
        return slice(j * LANES, (j + 1) * LANES)

    def own_total():
        return f_out[(ROWS - 1) * 16 : ROWS * 16, :]

    def place(values, iota, blocks):
        block = blocks
        for token, line in values:
            block = jnp.where(iota == token, line, block)
        return block

    def gate_up_part(h):
        load_rows(xr.at[h])
        for j in range(chunks):
            x_mat[h, :, part(j)] = columns(j * HALF, HALF)
        xm = x_mat[h]
        gate = dot(xm, wg[...], ((1,), (0,)))
        gu_part[:, :, 0:8, :] = gate.reshape(2, NZ, 8, width)
        up = dot(xm, wu[...], ((1,), (0,)))
        gu_part[:, :, 8:16, :] = up.reshape(2, NZ, 8, width)

        def give(m, carry):
            at = z_peer(m)
            gu_psend[h, at] = gu_part[1 - k, at].astype(BF16)
            remote(gu_psend.at[h, at], gu_precv.at[h, at], S_BP0 + h, partner, pair_sem.at[h, m])
            return carry

        lax.fori_loop(0, NZ, give, 0)

    def gate_up_scatter(h):
        def add(m):
            at = z_peer(m)
            pltpu.make_async_copy(gu_precv.at[h, 0], gu_precv.at[h, 0], pair_sem.at[h, m]).wait()
            return at, (gu_part[k, at] + gu_precv[h, at].astype(F32)).astype(BF16)

        def one(m, carry):
            at, total = add(m)
            gu_zsend[h, at] = total
            remote(gu_zsend.at[h, at], gu_zrecv.at[h, z], S_B0 + h, (row, at * 2 + k))
            return carry

        lax.fori_loop(0, NZ - 1, one, 0)
        gu_zrecv[h, z] = add(NZ - 1)[1]

    def hidden_spread(h):
        wait_recv(others(gu_zrecv.at[h], NZ), S_B0 + h)
        both = jnp.sum(gu_zrecv[h].astype(F32), axis=0)
        if h == 0:
            gu_keep[...] = both
        gate, up = both[0:8], both[8:16]
        hid = gate * jax.nn.sigmoid(gate) * up
        hc[h, k, z] = jnp.concatenate([hid[:, :half_width], hid[:, half_width:]], axis=0).astype(BF16)
        spread_z(hc.at[h], S_C0 + h)

    def hidden_matrix(h, core):
        v = hc[h, core].astype(F32)
        left = v[:, 0:8].reshape(TOK // 2, half_width).astype(BF16)
        right = v[:, 8:16].reshape(TOK // 2, half_width).astype(BF16)
        return jnp.concatenate([left, right], axis=1)

    def output_scatter(h):
        wait_recv(others(hc.at[h, 0], NZ), S_C0 + h)
        hm = hidden_matrix(h, k)
        if h == 0:
            h_mat[k] = hm
        for c in range(2):
            out = dot(hm, wd[c], ((1,), (0,)))
            for j in range(chunks):
                put_columns(out[:, part(j)], c * 8 + j * PAIR, PAIR)
        store_rows(y_send.at[h])
        y_keep[h] = own_total().reshape(2, 8, LANES)
        scatter_rows(y_send.at[h], y_recv.at[h], S_D0 + h)

    def output_total(h):
        wait_recv(y_recv.at[h], S_D0 + h)
        total = y_keep[h] + jnp.sum(y_recv[h].astype(F32), axis=0).reshape(2, 8, LANES)
        y_keep[h] = total.astype(BF16).astype(F32)

    spread_rows(xs.at[0], xr.at[0], S_A0)
    remote(tgt_give, tgt.at[k], S_TG, partner)
    for load in loads[4:]:
        load.wait()
    remote(wd.at[k], wd.at[k], S_WD, partner)
    wait_recv(others(xr.at[0], ROWS), S_A0)
    gate_up_part(0)
    gate_up_scatter(0)
    spread_rows(xs.at[1], xr.at[1], S_A1)
    hidden_spread(0)
    wait_recv(others(xr.at[1], ROWS), S_A1)
    gate_up_part(1)
    wait_recv(wd.at[0], S_WD)
    output_scatter(0)
    remote(hc.at[0, k], hc.at[0, k], S_CP, partner)
    gate_up_scatter(1)
    wait_recv(tgt_give, S_TG)
    output_total(0)

    gy = (0.25 * (y_keep[0] - tgt[...])).reshape(16, LANES).astype(BF16)
    gy_send[...] = gy
    gy_recv[ROWS - 1] = gy
    spread_rows(gy_send, gy_recv, S_E)
    hidden_spread(1)
    wait_recv(others(gy_recv, ROWS), S_E)

    load_rows(gy_recv)
    for j in range(chunks):
        gy_mat[k, :, part(j)] = columns(k * 8 + j * PAIR, PAIR)
        gy_give[:, part(j)] = columns((1 - k) * 8 + j * PAIR, PAIR)
    gh = dot(gy_mat[k], wd[k], ((1,), (1,))) + dot(gy_give[...], wd[1 - k], ((1,), (1,)))
    gh = gh.reshape(NZ, 8, width)
    gh = jnp.concatenate([gh[:, :, :half_width], gh[:, :, half_width:]], axis=1)
    gh_zsend[...] = gh.astype(BF16)
    gh_zrecv[z] = gh_zsend[z]
    scatter_z(gh_zsend, gh_zrecv, S_F)
    remote(gy_give, gy_mat.at[k], S_EP, partner)
    output_scatter(1)
    wait_recv(others(gh_zrecv, NZ), S_F)
    total = jnp.sum(gh_zrecv[...].astype(F32), axis=0)
    grad_hidden = jnp.concatenate([total[0:8], total[8:16]], axis=1)
    gate, up = gu_keep[0:8], gu_keep[8:16]
    sig = jax.nn.sigmoid(gate)
    gate_act = grad_hidden * up * sig * (1.0 + gate * (1.0 - sig))
    up_act = grad_hidden * gate * sig
    ac[k, z] = jnp.concatenate([gate_act, up_act], axis=0).astype(BF16)
    spread_z(ac, S_G, act_sem)
    remote(ac.at[k, z], ac.at[k, z], S_GP, partner)

    wait_recv(hc.at[0, 0], S_CP)
    wait_recv(gy_give, S_EP)
    h_mat[1 - k] = hidden_matrix(0, 1 - k)
    gd_out[...] = dot(
        h_mat[...].reshape(TOK, width), gy_mat[...].reshape(TOK, wide), ((0,), (0,))
    ).astype(BF16)
    stores[4].start()

    def pass_on(n, carry):
        m = NZ - 2 - n
        at = (z + NZ - zigzag(m, NZ)) % NZ
        pltpu.make_async_copy(ac.at[0, 0], ac.at[0, 0], act_sem.at[m]).wait()
        remote(ac.at[k, at], ac.at[k, at], S_GP, partner)
        return carry

    lax.fori_loop(0, NZ - 1, pass_on, 0)
    wait_recv(ac.at[0], S_GP)
    v = ac[...].astype(F32).reshape(2 * NZ, 16, width)
    act_mat[0] = v[:, 0:8].reshape(TOK, width).astype(BF16)
    act_mat[1] = v[:, 8:16].reshape(TOK, width).astype(BF16)
    grad = dot(act_mat[0], wg[...], ((1,), (1,))) + dot(act_mat[1], wu[...], ((1,), (1,)))
    for j in range(chunks):
        put_columns(grad[:, part(j)], j * HALF, HALF)
    store_rows(gt_send)
    scatter_rows(gt_send, gt_recv, S_H)

    output_total(1)
    for h in range(2):
        y_give[h] = y_keep[h, 1 - k]
    remote(y_give, y_take, S_Y, partner)
    gg_out[...] = dot(x_mat[0], act_mat[0], ((0,), (0,))).astype(BF16)
    stores[2].start()
    gu_out[...] = dot(x_mat[0], act_mat[1], ((0,), (0,))).astype(BF16)
    stores[3].start()
    wait_recv(y_give, S_Y)
    iota_t = lax.broadcasted_iota(jnp.int32, (2 * HALF, LANES), 0)
    zero = jnp.zeros((2 * HALF, LANES), F32)
    own, taken = [y_keep[h, k] for h in range(2)], [y_take[h] for h in range(2)]
    for j in range(chunks):
        values = []
        for h in range(2):
            for i in range(PAIR):
                at = j * PAIR + i
                low, high = pos[h][i], pos[h][PAIR + i]
                values.append((jnp.where(k == 0, low, high), own[h][at : at + 1]))
                values.append((jnp.where(k == 0, high, low), taken[h][at : at + 1]))
        y_out[:, part(j)] = place(values, iota_t, zero).astype(BF16)
    stores[0].start()
    wait_recv(gt_recv, S_H)
    total = own_total() + jnp.sum(gt_recv[...].astype(F32), axis=0)
    for j in range(chunks):
        values = [(pos[0][i], total[j * HALF + i : j * HALF + i + 1]) for i in range(HALF)]
        gt_out[:, part(j)] = place(values, iota_t, zero).astype(BF16)
    stores[1].start()

    for h in range(2):
        wait_send(others(xr.at[h], ROWS), S_A0 + h)
        wait_send(gu_precv.at[h], S_BP0 + h)
        wait_send(others(gu_zrecv.at[h], NZ), S_B0 + h)
        wait_send(others(hc.at[h, 0], NZ), S_C0 + h)
        wait_send(y_recv.at[h], S_D0 + h)
    wait_send(tgt_give, S_TG)
    wait_send(wd.at[0], S_WD)
    wait_send(hc.at[0, 0], S_CP)
    wait_send(others(gy_recv, ROWS), S_E)
    wait_send(gy_give, S_EP)
    wait_send(others(gh_zrecv, NZ), S_F)
    wait_send(others(ac.at[0], NZ), S_G)
    wait_send(ac.at[0], S_GP)
    wait_send(y_give, S_Y)
    wait_send(gt_recv, S_H)
    for store in stores:
        store.wait()


def write_out(*refs):
    sources, results, held, sem_in, sem_out = refs[0:5], refs[5:10], refs[10:15], refs[15], refs[16]
    reads, writes = [], []
    for src, dst, buf in zip(sources, results, held):
        rows = src.shape[0]
        step = rows // PIECES if rows >= 16 * PIECES else rows
        for at in range(0, rows, step):
            rng = pl.ds(at, step)
            n = len(reads)
            reads.append(pltpu.make_async_copy(src.at[rng], buf.at[rng], sem_in.at[n]))
            writes.append(pltpu.make_async_copy(buf.at[rng], dst.at[rng], sem_out.at[n]))
    for read in reads:
        read.start()
    for read, write in zip(reads, writes):
        read.wait()
        write.start()
    for write in writes:
        write.wait()


def on_device(tokens, w_gate, w_up, w_down, target_table, target_rows, buckets):
    wide, width = w_gate.shape
    half_width = width // 2
    hbm = pl.BlockSpec(memory_space=pltpu.HBM)
    outs = (tokens, tokens, w_gate, w_up, w_down)
    results = pl.pallas_call(
        kernel,
        out_shape=tuple(jax.ShapeDtypeStruct(a.shape, BF16) for a in outs),
        in_specs=[hbm] * 7,
        out_specs=(hbm,) * 5,
        scratch_shapes=[
            pltpu.SMEM(target_rows.shape, jnp.int32),
            pltpu.SMEM(buckets.shape, jnp.int32),
            pltpu.VMEM(tokens.shape, BF16),
            pltpu.VMEM(target_table.shape, BF16),
            pltpu.VMEM(w_gate.shape, BF16),
            pltpu.VMEM(w_up.shape, BF16),
            pltpu.VMEM((2, *w_down.shape), BF16),
            pltpu.VMEM((2, 16, LANES), BF16),
            pltpu.VMEM((2, ROWS, 16, LANES), BF16),
            pltpu.VMEM((ROWS * 16, LANES), F32),
            pltpu.VMEM((2, TOK, wide), BF16),
            pltpu.VMEM((2, NZ, 16, width), F32),
            pltpu.VMEM((2, NZ, 16, width), BF16),
            pltpu.VMEM((2, NZ, 16, width), BF16),
            pltpu.VMEM((2, NZ, 16, width), BF16),
            pltpu.VMEM((2, NZ, 16, width), BF16),
            pltpu.VMEM((16, width), F32),
            pltpu.VMEM((2, 2, NZ, 16, half_width), BF16),
            pltpu.VMEM((2, TOK // 2, width), BF16),
            pltpu.VMEM((ROWS * 16, LANES), F32),
            pltpu.VMEM((2, ROWS, 16, LANES), BF16),
            pltpu.VMEM((2, ROWS - 1, 16, LANES), BF16),
            pltpu.VMEM((2, 2, 8, LANES), F32),
            pltpu.VMEM((2, 8, LANES), F32),
            pltpu.VMEM((2, 8, LANES), F32),
            pltpu.VMEM((2, 8, LANES), F32),
            pltpu.VMEM((8, LANES), F32),
            pltpu.VMEM((16, LANES), BF16),
            pltpu.VMEM((ROWS, 16, LANES), BF16),
            pltpu.VMEM((2, TOK // 2, wide), BF16),
            pltpu.VMEM((TOK // 2, wide), BF16),
            pltpu.VMEM((NZ, 16, half_width), BF16),
            pltpu.VMEM((NZ, 16, half_width), BF16),
            pltpu.VMEM((2, NZ, 16, width), BF16),
            pltpu.VMEM((2, TOK, width), BF16),
            pltpu.VMEM((ROWS, 16, LANES), BF16),
            pltpu.VMEM((ROWS - 1, 16, LANES), BF16),
            *(pltpu.VMEM(a.shape, BF16) for a in outs),
            pltpu.SemaphoreType.DMA((NUM_SEMS,)),
            pltpu.SemaphoreType.DMA((NUM_SEMS,)),
            pltpu.SemaphoreType.DMA((7,)),
            pltpu.SemaphoreType.DMA((5,)),
            pltpu.SemaphoreType.DMA((2, NZ)),
            pltpu.SemaphoreType.DMA((NZ - 1,)),
        ],
        compiler_params=pltpu.CompilerParams(
            collective_id=0, has_side_effects=True, vmem_limit_bytes=VMEM_BYTES
        ),
        name="swiglu_step",
    )(target_rows, buckets, tokens, w_gate, w_up, w_down, target_table)
    return pl.pallas_call(
        write_out,
        out_shape=tuple(jax.ShapeDtypeStruct(a.shape, BF16) for a in outs),
        in_specs=[hbm] * 5,
        out_specs=(hbm,) * 5,
        scratch_shapes=[
            *(pltpu.VMEM(a.shape, BF16) for a in outs),
            pltpu.SemaphoreType.DMA((5 * PIECES,)),
            pltpu.SemaphoreType.DMA((5 * PIECES,)),
        ],
        compiler_params=pltpu.CompilerParams(vmem_limit_bytes=VMEM_BYTES),
        name="write_out",
    )(*results)


def solution(mesh):
    in_specs = (
        P("row", "col"),
        P("col", "row"),
        P("col", "row"),
        P("row", "col"),
        P(None, "col"),
        P("row"),
        P("row"),
    )
    out_specs = (
        P("row", "col"),
        P("row", "col"),
        P("col", "row"),
        P("col", "row"),
        P("row", "col"),
    )
    return jax.shard_map(
        on_device, mesh=mesh, in_specs=in_specs, out_specs=out_specs, check_vma=False
    )
```

```python
import jax
import jax.numpy as jnp
from jax import lax
from jax.experimental import pallas as pl
from jax.experimental.pallas import tpu as pltpu
from jax.sharding import PartitionSpec as P

VMEM_BYTES = 60 * 1024 * 1024
PIECES = 4
MESH = pl.DeviceIdType.MESH
BF16, F32 = jnp.bfloat16, jnp.float32

NY, NX, NZ = 8, 4, 8
ROWS = NY * NX
HALF = 4
LANES = 128
TOK = ROWS * HALF

(
    S_A0, S_A1, S_AO0, S_AO1, S_B0, S_B1, S_C0, S_C1, S_CP, S_D0, S_D1,
    S_E, S_EP, S_F, S_G, S_H, S_HO, S_WG, S_WU, S_WD, S_TG, S_Y, S_FC, S_X, S_AG, S_AU, NUM_SEMS,
) = range(27)
PAIR = HALF // 2


def zigzag(m, n):
    half = (m + 1) // 2
    return n // 2 + jnp.where(m % 2 == 0, half, -half)


def dot(left, right, dims):
    return lax.dot_general(left, right, ((dims[0], dims[1]), ((), ())), preferred_element_type=F32)


def kernel(
    rows_hbm, buckets_hbm, tokens_hbm, wg_hbm, wu_hbm, wd_hbm, table_hbm,
    y_hbm, gt_hbm, gg_hbm, gu_hbm, gd_hbm,
    rows_s, buckets_s, tokens_ref, table, wg, wu, wd,
    xs, xr, f_in, x_mat,
    x_full, gu_zsend, gu_zrecv,
    hc, h_mat,
    f_out, y_send, y_recv, y_keep, y_give, y_take, tgt, tgt_give,
    gy_send, gy_recv, gy_half, gy_mat,
    gh_zsend, gh_zrecv,
    fc, factor, ghc, act_mat, gt_send, gt_recv,
    y_out, gt_out, gg_out, gu_out, gd_out,
    send_sem, recv_sem, load_sem, store_sem,
):
    row, col = lax.axis_index("row"), lax.axis_index("col")
    y, x, z, k = row // NX, row % NX, col // 2, col % 2
    wide, width = wg.shape[1:]
    chunks = wide // LANES
    half_width = width // 2

    loads = [
        pltpu.make_async_copy(src, dst, load_sem.at[i])
        for i, (src, dst) in enumerate(
            [
                (rows_hbm, rows_s), (buckets_hbm, buckets_s), (tokens_hbm, tokens_ref), (table_hbm, table),
                (wg_hbm, wg.at[k]), (wu_hbm, wu.at[k]), (wd_hbm, wd.at[k]),
            ]
        )
    ]
    loads[0].start()
    loads[2].start()

    stores = [
        pltpu.make_async_copy(src, dst, store_sem.at[i])
        for i, (src, dst) in enumerate(
            [(y_out, y_hbm), (gt_out, gt_hbm), (gg_out, gg_hbm), (gu_out, gu_hbm), (gd_out, gd_hbm)]
        )
    ]

    def row_peer(m, sign, core=None):
        dy, dx = zigzag(m // NX, NY), zigzag(m % NX, NX)
        column = col if core is None else z * 2 + core
        return (((y + NY + sign * dy) % NY) * NX + (x + NX + sign * dx) % NX, column)

    def z_peer(m):
        return (z + zigzag(m, NZ)) % NZ

    partner = (row, z * 2 + 1 - k)

    barrier = pltpu.get_barrier_semaphore()

    def greet_row(m, carry):
        pl.semaphore_signal(barrier, inc=1, device_id=row_peer(m, 1, 1 - k), device_id_type=MESH)
        pl.semaphore_signal(barrier, inc=1, device_id=row_peer(m, 1), device_id_type=MESH)
        return carry

    def greet_col(m, carry):
        pl.semaphore_signal(barrier, inc=1, device_id=(row, z_peer(m) * 2 + k), device_id_type=MESH)
        return carry

    lax.fori_loop(0, ROWS - 1, greet_row, 0)
    lax.fori_loop(0, NZ - 1, greet_col, 0)
    pl.semaphore_signal(barrier, inc=1, device_id=partner, device_id_type=MESH)

    for i in (1, 3, 4, 5, 6):
        loads[i].start()
    loads[0].wait()
    loads[2].wait()
    tgt_pos = [rows_s[i] - 2 * HALF * row for i in range(HALF)]
    rest_pos = [jnp.int32(0)] * HALF
    seen = jnp.int32(0)
    for t in range(2 * HALF):
        is_target = jnp.int32(0)
        for p in tgt_pos:
            is_target = is_target + jnp.where(p == t, 1, 0)
        for i in range(HALF):
            rest_pos[i] = rest_pos[i] + jnp.where(seen == i, 1 - is_target, 0) * t
        seen = seen + 1 - is_target
    pos = [tgt_pos, rest_pos]

    tok = tokens_ref[...].astype(F32)
    iota8 = lax.broadcasted_iota(jnp.int32, tok.shape, 0)
    iota16 = lax.broadcasted_iota(jnp.int32, (16, LANES), 0)
    for h in range(2):
        packed = jnp.zeros((16, LANES), F32)
        for i in range(HALF):
            line = jnp.sum(jnp.where(iota8 == pos[h][i], tok, 0.0), axis=0, keepdims=True)
            for j in range(chunks):
                piece = line[:, j * LANES : (j + 1) * LANES]
                packed = jnp.where(iota16 == i // PAIR * 8 + j * PAIR + i % PAIR, piece, packed)
        for c in range(2):
            xs[h, c] = packed[c * 8 : c * 8 + 8].astype(BF16)
        xr[h, k, ROWS - 1] = xs[h, k]

    loads[1].wait()
    loads[3].wait()
    targets = jnp.zeros((16, LANES), F32)
    lane16 = lax.broadcasted_iota(jnp.int32, (16, table.shape[0]), 1)
    sub16 = lax.broadcasted_iota(jnp.int32, (16, table.shape[0]), 0)
    for j in range(chunks):
        onehot = jnp.zeros((16, table.shape[0]), F32)
        for i in range(HALF):
            at = i // PAIR * 8 + j * PAIR + i % PAIR
            hit = jnp.logical_and(sub16 == at, lane16 == buckets_s[i])
            onehot = jnp.where(hit, 1.0, onehot)
        targets = targets + dot(onehot.astype(BF16), table[:, j * LANES : (j + 1) * LANES], ((1,), (0,)))
    first = (jnp.zeros((8, LANES), jnp.int32) + k) == 0
    tgt[k] = jnp.where(first, targets[0:8], targets[8:16])
    tgt_give[...] = jnp.where(first, targets[8:16], targets[0:8])

    pl.semaphore_wait(barrier, 2 * (ROWS - 1) + NZ - 1 + 1)

    def wait_recv(ref, s):
        pltpu.make_async_copy(ref, ref, recv_sem.at[s]).wait()

    def wait_send(ref, s):
        pltpu.make_async_copy(ref, ref, send_sem.at[s]).wait()

    def remote(src, dst, s, device):
        pltpu.make_async_remote_copy(
            src_ref=src, dst_ref=dst, send_sem=send_sem.at[s], recv_sem=recv_sem.at[s],
            device_id=device, device_id_type=MESH,
        ).start()

    def spread_rows(src, dst, s):
        def one(m, carry):
            remote(src, dst.at[m], s, row_peer(m, 1))
            return carry

        lax.fori_loop(0, ROWS - 1, one, 0)

    def scatter_rows(src, dst, s):
        def one(m, carry):
            remote(src.at[m], dst.at[m], s, row_peer(m, -1))
            return carry

        lax.fori_loop(0, ROWS - 1, one, 0)

    def scatter_z(src, dst, s):
        def one(m, carry):
            peer = z_peer(m)
            remote(src.at[peer], dst.at[z], s, (row, peer * 2 + k))
            return carry

        lax.fori_loop(0, NZ - 1, one, 0)

    def spread_z(buf, s):
        def one(m, carry):
            here = buf.at[k, z]
            remote(here, here, s, (row, z_peer(m) * 2 + k))
            return carry

        lax.fori_loop(0, NZ - 1, one, 0)

    def others(buf, n):
        return buf.at[pl.ds(0, n - 1)]

    def load_rows(buf):
        f_in[...] = buf[...].astype(F32).reshape(ROWS * 16, LANES)

    def columns(at, step):
        parts = [f_in[pl.ds(at + i, ROWS, stride=step), :] for i in range(PAIR)]
        return jnp.concatenate(parts, axis=0).astype(BF16)

    def put_columns(mat, at, step):
        for i in range(PAIR):
            f_out[pl.ds(at + i, ROWS, stride=step), :] = mat[i * ROWS : (i + 1) * ROWS]

    def part(j):
        return slice(j * LANES, (j + 1) * LANES)

    def own_total():
        return f_out[(ROWS - 1) * 16 : ROWS * 16, :]

    def place(values, iota, blocks):
        block = blocks
        for token, line in values:
            block = jnp.where(iota == token, line, block)
        return block

    def tokens_spread(h):
        def one(m, carry):
            remote(xs.at[h, 1 - k], xr.at[h, k, m], S_AO0 + h, row_peer(m, 1, 1 - k))
            remote(xs.at[h, k], xr.at[h, k, m], S_A0 + h, row_peer(m, 1))
            return carry

        lax.fori_loop(0, ROWS - 1, one, 0)
        remote(xs.at[h, 1 - k], xr.at[h, k, ROWS - 1], S_AO0 + h, partner)

    def tokens_wait(h):
        wait_recv(others(xr.at[h, 0], ROWS), S_A0 + h)
        wait_recv(xr.at[h, 0], S_AO0 + h)

    def gate_up_scatter(h):
        load_rows(xr.at[h])
        for c in range(2):
            for j in range(chunks):
                x_mat[h, c, :, part(j)] = columns(c * ROWS * 8 + j * PAIR, 8)
        gate = dot(x_mat[h, 0], wg[0], ((1,), (0,))) + dot(x_mat[h, 1], wg[1], ((1,), (0,)))
        up = dot(x_mat[h, 0], wu[0], ((1,), (0,))) + dot(x_mat[h, 1], wu[1], ((1,), (0,)))
        gu_zsend[h, :, 0:16, :] = jnp.concatenate(
            [gate.reshape(NZ, 8, width), up.reshape(NZ, 8, width)], axis=1
        ).astype(BF16)
        gu_zrecv[h, z] = gu_zsend[h, z]
        scatter_z(gu_zsend.at[h], gu_zrecv.at[h], S_B0 + h)

    def hidden_spread(h):
        wait_recv(others(gu_zrecv.at[h], NZ), S_B0 + h)
        both = jnp.sum(gu_zrecv[h].astype(F32), axis=0)
        gate, up = both[0:8], both[8:16]
        sig = jax.nn.sigmoid(gate)
        hid = gate * sig * up
        hc[h, k, z] = jnp.concatenate([hid[:, :half_width], hid[:, half_width:]], axis=0).astype(BF16)
        spread_z(hc.at[h], S_C0 + h)
        if h == 0:
            gate_factor = up * sig * (1.0 + gate * (1.0 - sig))
            fc[k, z] = jnp.concatenate([gate_factor, gate * sig], axis=0).astype(BF16)

    def hidden_matrix(h, core):
        v = hc[h, core].astype(F32)
        left = v[:, 0:8].reshape(TOK // 2, half_width).astype(BF16)
        right = v[:, 8:16].reshape(TOK // 2, half_width).astype(BF16)
        return jnp.concatenate([left, right], axis=1)

    def output_scatter(h):
        wait_recv(others(hc.at[h, 0], NZ), S_C0 + h)
        hm = hidden_matrix(h, k)
        if h == 0:
            h_mat[k] = hm
        for c in range(2):
            out = dot(hm, wd[c], ((1,), (0,)))
            for j in range(chunks):
                put_columns(out[:, part(j)], c * 8 + j * PAIR, 16)
        y_send[h] = f_out[...].reshape(ROWS, 16, LANES).astype(BF16)
        y_keep[h] = own_total().reshape(2, 8, LANES)
        scatter_rows(y_send.at[h], y_recv.at[h], S_D0 + h)

    def output_total(h):
        wait_recv(y_recv.at[h], S_D0 + h)
        total = y_keep[h] + jnp.sum(y_recv[h].astype(F32), axis=0).reshape(2, 8, LANES)
        y_keep[h] = total.astype(BF16).astype(F32)

    tokens_spread(0)
    remote(tgt_give, tgt.at[k], S_TG, partner)
    for load in loads[4:]:
        load.wait()
    remote(wg.at[k], wg.at[k], S_WG, partner)
    remote(wu.at[k], wu.at[k], S_WU, partner)
    remote(wd.at[k], wd.at[k], S_WD, partner)
    tokens_wait(0)
    wait_recv(wg.at[0], S_WG)
    wait_recv(wu.at[0], S_WU)
    gate_up_scatter(0)
    tokens_spread(1)
    x_full[k] = x_mat[0, k]
    remote(x_mat.at[0, 1 - k], x_full.at[k], S_X, partner)
    hidden_spread(0)
    tokens_wait(1)
    wait_recv(wd.at[0], S_WD)
    output_scatter(0)
    remote(hc.at[0, k], hc.at[0, k], S_CP, partner)
    spread_z(fc, S_FC)
    gate_up_scatter(1)
    wait_recv(tgt_give, S_TG)
    output_total(0)

    gy = (0.25 * (y_keep[0] - tgt[...])).reshape(16, LANES).astype(BF16)
    gy_send[...] = gy
    gy_recv[ROWS - 1] = gy
    spread_rows(gy_send, gy_recv, S_E)
    hidden_spread(1)
    wait_recv(others(gy_recv, ROWS), S_E)

    load_rows(gy_recv)
    for j in range(chunks):
        for c in range(2):
            gy_half[c, :, part(j)] = columns(c * 8 + j * PAIR, 16)
    gh = dot(gy_half[0], wd[0], ((1,), (1,))) + dot(gy_half[1], wd[1], ((1,), (1,)))
    gh = gh.reshape(NZ, 8, width)
    gh = jnp.concatenate([gh[:, :, :half_width], gh[:, :, half_width:]], axis=1)
    gh_zsend[...] = gh.astype(BF16)
    gh_zrecv[z] = gh_zsend[z]
    scatter_z(gh_zsend, gh_zrecv, S_F)
    remote(gy_half.at[1 - k], gy_mat.at[k], S_EP, partner)
    gy_mat[k] = gy_half[k]
    wait_recv(others(fc.at[0], NZ), S_FC)
    v = fc[k].astype(F32)
    factor[0] = v[:, 0:8].reshape(TOK // 2, width)
    factor[1] = v[:, 8:16].reshape(TOK // 2, width)
    wait_recv(others(gh_zrecv, NZ), S_F)
    ghc[k, z] = jnp.sum(gh_zrecv[...].astype(F32), axis=0).astype(BF16)
    spread_z(ghc, S_G)

    output_scatter(1)

    wait_recv(others(ghc.at[0], NZ), S_G)
    v = ghc[k].astype(F32)
    for half in range(2):
        grad_hidden = v[:, half * 8 : half * 8 + 8].reshape(TOK // 2, half_width)
        cols = slice(half * half_width, (half + 1) * half_width)
        for i in range(2):
            act_mat[i, k, :, cols] = (grad_hidden * factor[i, :, cols]).astype(BF16)
    gate_act, up_act = act_mat[0, k], act_mat[1, k]
    for c in range(2):
        grad = dot(gate_act, wg[c], ((1,), (1,))) + dot(up_act, wu[c], ((1,), (1,)))
        for j in range(chunks):
            put_columns(grad[:, part(j)], c * ROWS * 8 + j * PAIR, 8)
    gt_send[...] = f_out[...].reshape(2, ROWS, 8, LANES).astype(BF16)
    gt_recv[k, ROWS - 1] = gt_send[k, ROWS - 1]

    def grad_out(m, carry):
        remote(gt_send.at[1 - k, m], gt_recv.at[k, m], S_HO, row_peer(m, -1, 1 - k))
        remote(gt_send.at[k, m], gt_recv.at[k, m], S_H, row_peer(m, -1))
        return carry

    lax.fori_loop(0, ROWS - 1, grad_out, 0)
    remote(gt_send.at[1 - k, ROWS - 1], gt_recv.at[k, ROWS - 1], S_HO, partner)
    remote(act_mat.at[0, k], act_mat.at[0, k], S_AG, partner)
    remote(act_mat.at[1, k], act_mat.at[1, k], S_AU, partner)

    wait_recv(hc.at[0, 0], S_CP)
    wait_recv(gy_mat.at[0], S_EP)
    h_mat[1 - k] = hidden_matrix(0, 1 - k)
    gd_out[...] = dot(
        h_mat[...].reshape(TOK, width), gy_mat[...].reshape(TOK, wide), ((0,), (0,))
    ).astype(BF16)
    stores[4].start()
    output_total(1)
    for h in range(2):
        y_give[h] = y_keep[h, 1 - k]
    remote(y_give, y_take, S_Y, partner)
    wait_recv(x_full.at[0], S_X)
    wait_recv(act_mat.at[0, 0], S_AG)
    wait_recv(act_mat.at[1, 0], S_AU)
    xm = x_full[...].reshape(TOK, wide)
    gg_out[...] = dot(xm, act_mat[0].reshape(TOK, width), ((0,), (0,))).astype(BF16)
    stores[2].start()
    gu_out[...] = dot(xm, act_mat[1].reshape(TOK, width), ((0,), (0,))).astype(BF16)
    stores[3].start()
    wait_recv(y_give, S_Y)
    iota_t = lax.broadcasted_iota(jnp.int32, (2 * HALF, LANES), 0)
    zero = jnp.zeros((2 * HALF, LANES), F32)
    own, taken = [y_keep[h, k] for h in range(2)], [y_take[h] for h in range(2)]
    for j in range(chunks):
        values = []
        for h in range(2):
            for i in range(PAIR):
                at = j * PAIR + i
                low, high = pos[h][i], pos[h][PAIR + i]
                values.append((jnp.where(k == 0, low, high), own[h][at : at + 1]))
                values.append((jnp.where(k == 0, high, low), taken[h][at : at + 1]))
        y_out[:, part(j)] = place(values, iota_t, zero).astype(BF16)
    stores[0].start()
    wait_recv(others(gt_recv.at[0], ROWS), S_H)
    wait_recv(gt_recv.at[0], S_HO)
    totals = [jnp.sum(gt_recv[c].astype(F32), axis=0) for c in range(2)]
    for j in range(chunks):
        values = []
        for i in range(HALF):
            at = j * PAIR + i % PAIR
            values.append((pos[0][i], totals[i // PAIR][at : at + 1]))
        gt_out[:, part(j)] = place(values, iota_t, zero).astype(BF16)
    stores[1].start()

    for h in range(2):
        wait_send(others(xr.at[h, 0], ROWS), S_A0 + h)
        wait_send(xr.at[h, 0], S_AO0 + h)
        wait_send(others(gu_zrecv.at[h], NZ), S_B0 + h)
        wait_send(others(hc.at[h, 0], NZ), S_C0 + h)
        wait_send(y_recv.at[h], S_D0 + h)
    wait_send(tgt_give, S_TG)
    wait_send(wd.at[0], S_WD)
    wait_send(hc.at[0, 0], S_CP)
    wait_send(others(gy_recv, ROWS), S_E)
    wait_send(gy_mat.at[0], S_EP)
    wait_send(others(gh_zrecv, NZ), S_F)
    wait_send(others(ghc.at[0], NZ), S_G)
    wait_send(others(fc.at[0], NZ), S_FC)
    wait_send(wg.at[0], S_WG)
    wait_send(wu.at[0], S_WU)
    wait_send(x_full.at[0], S_X)
    wait_send(act_mat.at[0, 0], S_AG)
    wait_send(act_mat.at[1, 0], S_AU)
    wait_send(y_give, S_Y)
    wait_send(others(gt_recv.at[0], ROWS), S_H)
    wait_send(gt_recv.at[0], S_HO)
    for store in stores:
        store.wait()


def write_out(*refs):
    sources, results, held, sem_in, sem_out = refs[0:5], refs[5:10], refs[10:15], refs[15], refs[16]
    reads, writes = [], []
    for src, dst, buf in zip(sources, results, held):
        rows = src.shape[0]
        step = rows // PIECES if rows >= 16 * PIECES else rows
        for at in range(0, rows, step):
            rng = pl.ds(at, step)
            n = len(reads)
            reads.append(pltpu.make_async_copy(src.at[rng], buf.at[rng], sem_in.at[n]))
            writes.append(pltpu.make_async_copy(buf.at[rng], dst.at[rng], sem_out.at[n]))
    for read in reads:
        read.start()
    for read, write in zip(reads, writes):
        read.wait()
        write.start()
    for write in writes:
        write.wait()


def on_device(tokens, w_gate, w_up, w_down, target_table, target_rows, buckets):
    wide, width = w_gate.shape
    half_width = width // 2
    hbm = pl.BlockSpec(memory_space=pltpu.HBM)
    outs = (tokens, tokens, w_gate, w_up, w_down)
    results = pl.pallas_call(
        kernel,
        out_shape=tuple(jax.ShapeDtypeStruct(a.shape, BF16) for a in outs),
        in_specs=[hbm] * 7,
        out_specs=(hbm,) * 5,
        scratch_shapes=[
            pltpu.SMEM(target_rows.shape, jnp.int32),
            pltpu.SMEM(buckets.shape, jnp.int32),
            pltpu.VMEM(tokens.shape, BF16),
            pltpu.VMEM(target_table.shape, BF16),
            pltpu.VMEM((2, *w_gate.shape), BF16),
            pltpu.VMEM((2, *w_up.shape), BF16),
            pltpu.VMEM((2, *w_down.shape), BF16),
            pltpu.VMEM((2, 2, 8, LANES), BF16),
            pltpu.VMEM((2, 2, ROWS, 8, LANES), BF16),
            pltpu.VMEM((ROWS * 16, LANES), F32),
            pltpu.VMEM((2, 2, TOK // 2, wide), BF16),
            pltpu.VMEM((2, TOK // 2, wide), BF16),
            pltpu.VMEM((2, NZ, 16, width), BF16),
            pltpu.VMEM((2, NZ, 16, width), BF16),
            pltpu.VMEM((2, 2, NZ, 16, half_width), BF16),
            pltpu.VMEM((2, TOK // 2, width), BF16),
            pltpu.VMEM((ROWS * 16, LANES), F32),
            pltpu.VMEM((2, ROWS, 16, LANES), BF16),
            pltpu.VMEM((2, ROWS - 1, 16, LANES), BF16),
            pltpu.VMEM((2, 2, 8, LANES), F32),
            pltpu.VMEM((2, 8, LANES), F32),
            pltpu.VMEM((2, 8, LANES), F32),
            pltpu.VMEM((2, 8, LANES), F32),
            pltpu.VMEM((8, LANES), F32),
            pltpu.VMEM((16, LANES), BF16),
            pltpu.VMEM((ROWS, 16, LANES), BF16),
            pltpu.VMEM((2, TOK // 2, wide), BF16),
            pltpu.VMEM((2, TOK // 2, wide), BF16),
            pltpu.VMEM((NZ, 16, half_width), BF16),
            pltpu.VMEM((NZ, 16, half_width), BF16),
            pltpu.VMEM((2, NZ, 16, width), BF16),
            pltpu.VMEM((2, TOK // 2, width), F32),
            pltpu.VMEM((2, NZ, 16, half_width), BF16),
            pltpu.VMEM((2, 2, TOK // 2, width), BF16),
            pltpu.VMEM((2, ROWS, 8, LANES), BF16),
            pltpu.VMEM((2, ROWS, 8, LANES), BF16),
            *(pltpu.VMEM(a.shape, BF16) for a in outs),
            pltpu.SemaphoreType.DMA((NUM_SEMS,)),
            pltpu.SemaphoreType.DMA((NUM_SEMS,)),
            pltpu.SemaphoreType.DMA((7,)),
            pltpu.SemaphoreType.DMA((5,)),
        ],
        compiler_params=pltpu.CompilerParams(
            collective_id=0, has_side_effects=True, vmem_limit_bytes=VMEM_BYTES
        ),
        name="swiglu_step",
    )(target_rows, buckets, tokens, w_gate, w_up, w_down, target_table)
    return pl.pallas_call(
        write_out,
        out_shape=tuple(jax.ShapeDtypeStruct(a.shape, BF16) for a in outs),
        in_specs=[hbm] * 5,
        out_specs=(hbm,) * 5,
        scratch_shapes=[
            *(pltpu.VMEM(a.shape, BF16) for a in outs),
            pltpu.SemaphoreType.DMA((5 * PIECES,)),
            pltpu.SemaphoreType.DMA((5 * PIECES,)),
        ],
        compiler_params=pltpu.CompilerParams(vmem_limit_bytes=VMEM_BYTES),
        name="write_out",
    )(*results)


def solution(mesh):
    in_specs = (
        P("row", "col"),
        P("col", "row"),
        P("col", "row"),
        P("row", "col"),
        P(None, "col"),
        P("row"),
        P("row"),
    )
    out_specs = (
        P("row", "col"),
        P("row", "col"),
        P("col", "row"),
        P("col", "row"),
        P("row", "col"),
    )
    return jax.shard_map(
        on_device, mesh=mesh, in_specs=in_specs, out_specs=out_specs, check_vma=False
    )
```

```python
import jax
import jax.numpy as jnp
from jax import lax
from jax.experimental import pallas as pl
from jax.experimental.pallas import tpu as pltpu
from jax.sharding import PartitionSpec as P

VMEM_BYTES = 60 * 1024 * 1024
PIECES = 4
MESH = pl.DeviceIdType.MESH
BF16, F32 = jnp.bfloat16, jnp.float32

NY, NX, NZ = 8, 4, 8
ROWS = NY * NX
HALF = 4
LANES = 128
TOK = ROWS * HALF

(
    S_A0, S_A1, S_AO0, S_AO1, S_B0, S_B1, S_C0, S_C1, S_CP, S_D0, S_D1,
    S_E, S_EP, S_F, S_G, S_H, S_HO, S_WG, S_WU, S_WD, S_TG, S_Y, S_FC, S_X, S_AG, S_AU, NUM_SEMS,
) = range(27)
PAIR = HALF // 2


def zigzag(m, n):
    half = (m + 1) // 2
    return n // 2 + jnp.where(m % 2 == 0, half, -half)


def dot(left, right, dims):
    return lax.dot_general(left, right, ((dims[0], dims[1]), ((), ())), preferred_element_type=F32)


def kernel(
    rows_hbm, buckets_hbm, tokens_hbm, wg_hbm, wu_hbm, wd_hbm, table_hbm,
    y_hbm, gt_hbm, gg_hbm, gu_hbm, gd_hbm,
    rows_s, buckets_s, tokens_ref, table, wg, wu, wd,
    xs, xr, f_in, x_mat,
    x_full, gu_zsend, gu_zrecv,
    hc, h_mat,
    f_out, y_send, y_recv, y_keep, y_give, y_take, tgt, tgt_give,
    gy_send, gy_recv, gy_half, gy_mat,
    gh_zsend, gh_zrecv,
    fc, factor, ghc, act_mat, gt_send, gt_recv,
    y_out, gt_out, gg_out, gu_out, gd_out,
    send_sem, recv_sem, load_sem, store_sem,
):
    row, col = lax.axis_index("row"), lax.axis_index("col")
    y, x, z, k = row // NX, row % NX, col // 2, col % 2
    wide, width = wg.shape[1:]
    chunks = wide // LANES
    half_width = width // 2

    loads = [
        pltpu.make_async_copy(src, dst, load_sem.at[i])
        for i, (src, dst) in enumerate(
            [
                (rows_hbm, rows_s), (buckets_hbm, buckets_s), (tokens_hbm, tokens_ref), (table_hbm, table),
                (wg_hbm, wg.at[k]), (wu_hbm, wu.at[k]), (wd_hbm, wd.at[k]),
            ]
        )
    ]
    loads[0].start()
    loads[2].start()

    stores = [
        pltpu.make_async_copy(src, dst, store_sem.at[i])
        for i, (src, dst) in enumerate(
            [(y_out, y_hbm), (gt_out, gt_hbm), (gg_out, gg_hbm), (gu_out, gu_hbm), (gd_out, gd_hbm)]
        )
    ]

    def row_peer(m, sign, core=None):
        dy, dx = zigzag(m // NX, NY), zigzag(m % NX, NX)
        column = col if core is None else z * 2 + core
        return (((y + NY + sign * dy) % NY) * NX + (x + NX + sign * dx) % NX, column)

    def z_peer(m):
        return (z + zigzag(m, NZ)) % NZ

    partner = (row, z * 2 + 1 - k)

    barrier = pltpu.get_barrier_semaphore()

    def greet_row(m, carry):
        pl.semaphore_signal(barrier, inc=1, device_id=row_peer(m, 1, 1 - k), device_id_type=MESH)
        pl.semaphore_signal(barrier, inc=1, device_id=row_peer(m, 1), device_id_type=MESH)
        return carry

    def greet_col(m, carry):
        pl.semaphore_signal(barrier, inc=1, device_id=(row, z_peer(m) * 2 + k), device_id_type=MESH)
        return carry

    lax.fori_loop(0, ROWS - 1, greet_row, 0)
    lax.fori_loop(0, NZ - 1, greet_col, 0)
    pl.semaphore_signal(barrier, inc=1, device_id=partner, device_id_type=MESH)

    for i in (1, 3, 4, 5, 6):
        loads[i].start()
    loads[0].wait()
    loads[2].wait()
    tgt_pos = [rows_s[i] - 2 * HALF * row for i in range(HALF)]
    rest_pos = [jnp.int32(0)] * HALF
    seen = jnp.int32(0)
    for t in range(2 * HALF):
        is_target = jnp.int32(0)
        for p in tgt_pos:
            is_target = is_target + jnp.where(p == t, 1, 0)
        for i in range(HALF):
            rest_pos[i] = rest_pos[i] + jnp.where(seen == i, 1 - is_target, 0) * t
        seen = seen + 1 - is_target
    pos = [tgt_pos, rest_pos]

    tok = tokens_ref[...].astype(F32)
    iota8 = lax.broadcasted_iota(jnp.int32, tok.shape, 0)
    iota16 = lax.broadcasted_iota(jnp.int32, (16, LANES), 0)
    for h in range(2):
        packed = jnp.zeros((16, LANES), F32)
        for i in range(HALF):
            line = jnp.sum(jnp.where(iota8 == pos[h][i], tok, 0.0), axis=0, keepdims=True)
            for j in range(chunks):
                piece = line[:, j * LANES : (j + 1) * LANES]
                packed = jnp.where(iota16 == i // PAIR * 8 + j * PAIR + i % PAIR, piece, packed)
        for c in range(2):
            xs[h, c] = packed[c * 8 : c * 8 + 8].astype(BF16)
        xr[h, k, ROWS - 1] = xs[h, k]

    loads[1].wait()
    loads[3].wait()
    targets = jnp.zeros((16, LANES), F32)
    lane16 = lax.broadcasted_iota(jnp.int32, (16, table.shape[0]), 1)
    sub16 = lax.broadcasted_iota(jnp.int32, (16, table.shape[0]), 0)
    for j in range(chunks):
        onehot = jnp.zeros((16, table.shape[0]), F32)
        for i in range(HALF):
            at = i // PAIR * 8 + j * PAIR + i % PAIR
            hit = jnp.logical_and(sub16 == at, lane16 == buckets_s[i])
            onehot = jnp.where(hit, 1.0, onehot)
        targets = targets + dot(onehot.astype(BF16), table[:, j * LANES : (j + 1) * LANES], ((1,), (0,)))
    first = (jnp.zeros((8, LANES), jnp.int32) + k) == 0
    tgt[k] = jnp.where(first, targets[0:8], targets[8:16])
    tgt_give[...] = jnp.where(first, targets[8:16], targets[0:8])

    pl.semaphore_wait(barrier, 2 * (ROWS - 1) + NZ - 1 + 1)

    def wait_recv(ref, s):
        pltpu.make_async_copy(ref, ref, recv_sem.at[s]).wait()

    def wait_send(ref, s):
        pltpu.make_async_copy(ref, ref, send_sem.at[s]).wait()

    def remote(src, dst, s, device):
        pltpu.make_async_remote_copy(
            src_ref=src, dst_ref=dst, send_sem=send_sem.at[s], recv_sem=recv_sem.at[s],
            device_id=device, device_id_type=MESH,
        ).start()

    def spread_rows(src, dst, s):
        def one(m, carry):
            remote(src, dst.at[m], s, row_peer(m, 1))
            return carry

        lax.fori_loop(0, ROWS - 1, one, 0)

    def scatter_rows(src, dst, s):
        def one(m, carry):
            remote(src.at[m], dst.at[m], s, row_peer(m, -1))
            return carry

        lax.fori_loop(0, ROWS - 1, one, 0)

    def scatter_z(src, dst, s):
        def one(m, carry):
            peer = z_peer(m)
            remote(src.at[peer], dst.at[z], s, (row, peer * 2 + k))
            return carry

        lax.fori_loop(0, NZ - 1, one, 0)

    def spread_z(buf, s):
        def one(m, carry):
            here = buf.at[k, z]
            remote(here, here, s, (row, z_peer(m) * 2 + k))
            return carry

        lax.fori_loop(0, NZ - 1, one, 0)

    def others(buf, n):
        return buf.at[pl.ds(0, n - 1)]

    def load_rows(buf):
        f_in[...] = buf[...].astype(F32).reshape(ROWS * 16, LANES)

    def columns(at, step):
        parts = [f_in[pl.ds(at + i, ROWS, stride=step), :] for i in range(PAIR)]
        return jnp.concatenate(parts, axis=0).astype(BF16)

    def put_columns(mat, at, step):
        for i in range(PAIR):
            f_out[pl.ds(at + i, ROWS, stride=step), :] = mat[i * ROWS : (i + 1) * ROWS]

    def part(j):
        return slice(j * LANES, (j + 1) * LANES)

    def own_total():
        return f_out[(ROWS - 1) * 16 : ROWS * 16, :]

    def place(values, iota, blocks):
        block = blocks
        for token, line in values:
            block = jnp.where(iota == token, line, block)
        return block

    def tokens_spread(h):
        def one(m, carry):
            remote(xs.at[h, 1 - k], xr.at[h, k, m], S_AO0 + h, row_peer(m, 1, 1 - k))
            return carry

        def two(m, carry):
            remote(xs.at[h, k], xr.at[h, k, m], S_A0 + h, row_peer(m, 1))
            return carry

        lax.fori_loop(0, ROWS - 1, one, 0)
        lax.fori_loop(0, ROWS - 1, two, 0)
        remote(xs.at[h, 1 - k], xr.at[h, k, ROWS - 1], S_AO0 + h, partner)

    def tokens_wait(h):
        wait_recv(others(xr.at[h, 0], ROWS), S_A0 + h)
        wait_recv(xr.at[h, 0], S_AO0 + h)

    def gate_up_scatter(h):
        load_rows(xr.at[h])
        for c in range(2):
            for j in range(chunks):
                x_mat[h, c, :, part(j)] = columns(c * ROWS * 8 + j * PAIR, 8)
        gate = dot(x_mat[h, 0], wg[0], ((1,), (0,))) + dot(x_mat[h, 1], wg[1], ((1,), (0,)))
        up = dot(x_mat[h, 0], wu[0], ((1,), (0,))) + dot(x_mat[h, 1], wu[1], ((1,), (0,)))
        gu_zsend[h, :, 0:16, :] = jnp.concatenate(
            [gate.reshape(NZ, 8, width), up.reshape(NZ, 8, width)], axis=1
        ).astype(BF16)
        gu_zrecv[h, z] = gu_zsend[h, z]
        scatter_z(gu_zsend.at[h], gu_zrecv.at[h], S_B0 + h)

    def hidden_spread(h):
        wait_recv(others(gu_zrecv.at[h], NZ), S_B0 + h)
        both = jnp.sum(gu_zrecv[h].astype(F32), axis=0)
        gate, up = both[0:8], both[8:16]
        sig = jax.nn.sigmoid(gate)
        hid = gate * sig * up
        hc[h, k, z] = jnp.concatenate([hid[:, :half_width], hid[:, half_width:]], axis=0).astype(BF16)
        spread_z(hc.at[h], S_C0 + h)
        if h == 0:
            gate_factor = up * sig * (1.0 + gate * (1.0 - sig))
            fc[k, z] = jnp.concatenate([gate_factor, gate * sig], axis=0).astype(BF16)

    def hidden_matrix(h, core):
        v = hc[h, core].astype(F32)
        left = v[:, 0:8].reshape(TOK // 2, half_width).astype(BF16)
        right = v[:, 8:16].reshape(TOK // 2, half_width).astype(BF16)
        return jnp.concatenate([left, right], axis=1)

    def output_scatter(h):
        wait_recv(others(hc.at[h, 0], NZ), S_C0 + h)
        hm = hidden_matrix(h, k)
        if h == 0:
            h_mat[k] = hm
        for c in range(2):
            out = dot(hm, wd[c], ((1,), (0,)))
            for j in range(chunks):
                put_columns(out[:, part(j)], c * 8 + j * PAIR, 16)
        y_send[h] = f_out[...].reshape(ROWS, 16, LANES).astype(BF16)
        y_keep[h] = own_total().reshape(2, 8, LANES)
        scatter_rows(y_send.at[h], y_recv.at[h], S_D0 + h)

    def output_total(h):
        wait_recv(y_recv.at[h], S_D0 + h)
        total = y_keep[h] + jnp.sum(y_recv[h].astype(F32), axis=0).reshape(2, 8, LANES)
        y_keep[h] = total.astype(BF16).astype(F32)

    tokens_spread(0)
    remote(tgt_give, tgt.at[k], S_TG, partner)
    for load in loads[4:]:
        load.wait()
    remote(wg.at[k], wg.at[k], S_WG, partner)
    remote(wu.at[k], wu.at[k], S_WU, partner)
    remote(wd.at[k], wd.at[k], S_WD, partner)
    tokens_wait(0)
    wait_recv(wg.at[0], S_WG)
    wait_recv(wu.at[0], S_WU)
    gate_up_scatter(0)
    tokens_spread(1)
    x_full[k] = x_mat[0, k]
    remote(x_mat.at[0, 1 - k], x_full.at[k], S_X, partner)
    hidden_spread(0)
    tokens_wait(1)
    wait_recv(wd.at[0], S_WD)
    output_scatter(0)
    remote(hc.at[0, k], hc.at[0, k], S_CP, partner)
    spread_z(fc, S_FC)
    gate_up_scatter(1)
    wait_recv(tgt_give, S_TG)
    output_total(0)

    gy = (0.25 * (y_keep[0] - tgt[...])).reshape(16, LANES).astype(BF16)
    gy_send[...] = gy
    gy_recv[ROWS - 1] = gy
    spread_rows(gy_send, gy_recv, S_E)
    hidden_spread(1)
    wait_recv(others(gy_recv, ROWS), S_E)

    load_rows(gy_recv)
    for j in range(chunks):
        for c in range(2):
            gy_half[c, :, part(j)] = columns(c * 8 + j * PAIR, 16)
    gh = dot(gy_half[0], wd[0], ((1,), (1,))) + dot(gy_half[1], wd[1], ((1,), (1,)))
    gh = gh.reshape(NZ, 8, width)
    gh = jnp.concatenate([gh[:, :, :half_width], gh[:, :, half_width:]], axis=1)
    gh_zsend[...] = gh.astype(BF16)
    gh_zrecv[z] = gh_zsend[z]
    scatter_z(gh_zsend, gh_zrecv, S_F)
    remote(gy_half.at[1 - k], gy_mat.at[k], S_EP, partner)
    gy_mat[k] = gy_half[k]
    wait_recv(others(fc.at[0], NZ), S_FC)
    v = fc[k].astype(F32)
    factor[0] = v[:, 0:8].reshape(TOK // 2, width)
    factor[1] = v[:, 8:16].reshape(TOK // 2, width)
    wait_recv(others(gh_zrecv, NZ), S_F)
    ghc[k, z] = jnp.sum(gh_zrecv[...].astype(F32), axis=0).astype(BF16)
    spread_z(ghc, S_G)

    output_scatter(1)

    wait_recv(others(ghc.at[0], NZ), S_G)
    v = ghc[k].astype(F32)
    for half in range(2):
        grad_hidden = v[:, half * 8 : half * 8 + 8].reshape(TOK // 2, half_width)
        cols = slice(half * half_width, (half + 1) * half_width)
        for i in range(2):
            act_mat[i, k, :, cols] = (grad_hidden * factor[i, :, cols]).astype(BF16)
    gate_act, up_act = act_mat[0, k], act_mat[1, k]
    for c in range(2):
        grad = dot(gate_act, wg[c], ((1,), (1,))) + dot(up_act, wu[c], ((1,), (1,)))
        for j in range(chunks):
            put_columns(grad[:, part(j)], c * ROWS * 8 + j * PAIR, 8)
    gt_send[...] = f_out[...].reshape(2, ROWS, 8, LANES).astype(BF16)
    gt_recv[k, ROWS - 1] = gt_send[k, ROWS - 1]

    def grad_out(m, carry):
        remote(gt_send.at[1 - k, m], gt_recv.at[k, m], S_HO, row_peer(m, -1, 1 - k))
        return carry

    def grad_own(m, carry):
        remote(gt_send.at[k, m], gt_recv.at[k, m], S_H, row_peer(m, -1))
        return carry

    lax.fori_loop(0, ROWS - 1, grad_out, 0)
    lax.fori_loop(0, ROWS - 1, grad_own, 0)
    remote(gt_send.at[1 - k, ROWS - 1], gt_recv.at[k, ROWS - 1], S_HO, partner)
    remote(act_mat.at[0, k], act_mat.at[0, k], S_AG, partner)
    remote(act_mat.at[1, k], act_mat.at[1, k], S_AU, partner)

    wait_recv(hc.at[0, 0], S_CP)
    wait_recv(gy_mat.at[0], S_EP)
    h_mat[1 - k] = hidden_matrix(0, 1 - k)
    gd_out[...] = dot(
        h_mat[...].reshape(TOK, width), gy_mat[...].reshape(TOK, wide), ((0,), (0,))
    ).astype(BF16)
    stores[4].start()
    output_total(1)
    for h in range(2):
        y_give[h] = y_keep[h, 1 - k]
    remote(y_give, y_take, S_Y, partner)
    wait_recv(x_full.at[0], S_X)
    wait_recv(act_mat.at[0, 0], S_AG)
    wait_recv(act_mat.at[1, 0], S_AU)
    xm = x_full[...].reshape(TOK, wide)
    gg_out[...] = dot(xm, act_mat[0].reshape(TOK, width), ((0,), (0,))).astype(BF16)
    stores[2].start()
    gu_out[...] = dot(xm, act_mat[1].reshape(TOK, width), ((0,), (0,))).astype(BF16)
    stores[3].start()
    wait_recv(y_give, S_Y)
    iota_t = lax.broadcasted_iota(jnp.int32, (2 * HALF, LANES), 0)
    zero = jnp.zeros((2 * HALF, LANES), F32)
    own, taken = [y_keep[h, k] for h in range(2)], [y_take[h] for h in range(2)]
    for j in range(chunks):
        values = []
        for h in range(2):
            for i in range(PAIR):
                at = j * PAIR + i
                low, high = pos[h][i], pos[h][PAIR + i]
                values.append((jnp.where(k == 0, low, high), own[h][at : at + 1]))
                values.append((jnp.where(k == 0, high, low), taken[h][at : at + 1]))
        y_out[:, part(j)] = place(values, iota_t, zero).astype(BF16)
    stores[0].start()
    wait_recv(others(gt_recv.at[0], ROWS), S_H)
    wait_recv(gt_recv.at[0], S_HO)
    totals = [jnp.sum(gt_recv[c].astype(F32), axis=0) for c in range(2)]
    for j in range(chunks):
        values = []
        for i in range(HALF):
            at = j * PAIR + i % PAIR
            values.append((pos[0][i], totals[i // PAIR][at : at + 1]))
        gt_out[:, part(j)] = place(values, iota_t, zero).astype(BF16)
    stores[1].start()

    for h in range(2):
        wait_send(others(xr.at[h, 0], ROWS), S_A0 + h)
        wait_send(xr.at[h, 0], S_AO0 + h)
        wait_send(others(gu_zrecv.at[h], NZ), S_B0 + h)
        wait_send(others(hc.at[h, 0], NZ), S_C0 + h)
        wait_send(y_recv.at[h], S_D0 + h)
    wait_send(tgt_give, S_TG)
    wait_send(wd.at[0], S_WD)
    wait_send(hc.at[0, 0], S_CP)
    wait_send(others(gy_recv, ROWS), S_E)
    wait_send(gy_mat.at[0], S_EP)
    wait_send(others(gh_zrecv, NZ), S_F)
    wait_send(others(ghc.at[0], NZ), S_G)
    wait_send(others(fc.at[0], NZ), S_FC)
    wait_send(wg.at[0], S_WG)
    wait_send(wu.at[0], S_WU)
    wait_send(x_full.at[0], S_X)
    wait_send(act_mat.at[0, 0], S_AG)
    wait_send(act_mat.at[1, 0], S_AU)
    wait_send(y_give, S_Y)
    wait_send(others(gt_recv.at[0], ROWS), S_H)
    wait_send(gt_recv.at[0], S_HO)
    for store in stores:
        store.wait()


def write_out(*refs):
    sources, results, held, sem_in, sem_out = refs[0:5], refs[5:10], refs[10:15], refs[15], refs[16]
    reads, writes = [], []
    for src, dst, buf in zip(sources, results, held):
        rows = src.shape[0]
        step = rows // PIECES if rows >= 16 * PIECES else rows
        for at in range(0, rows, step):
            rng = pl.ds(at, step)
            n = len(reads)
            reads.append(pltpu.make_async_copy(src.at[rng], buf.at[rng], sem_in.at[n]))
            writes.append(pltpu.make_async_copy(buf.at[rng], dst.at[rng], sem_out.at[n]))
    for read in reads:
        read.start()
    for read, write in zip(reads, writes):
        read.wait()
        write.start()
    for write in writes:
        write.wait()


def on_device(tokens, w_gate, w_up, w_down, target_table, target_rows, buckets):
    wide, width = w_gate.shape
    half_width = width // 2
    hbm = pl.BlockSpec(memory_space=pltpu.HBM)
    outs = (tokens, tokens, w_gate, w_up, w_down)
    results = pl.pallas_call(
        kernel,
        out_shape=tuple(jax.ShapeDtypeStruct(a.shape, BF16) for a in outs),
        in_specs=[hbm] * 7,
        out_specs=(hbm,) * 5,
        scratch_shapes=[
            pltpu.SMEM(target_rows.shape, jnp.int32),
            pltpu.SMEM(buckets.shape, jnp.int32),
            pltpu.VMEM(tokens.shape, BF16),
            pltpu.VMEM(target_table.shape, BF16),
            pltpu.VMEM((2, *w_gate.shape), BF16),
            pltpu.VMEM((2, *w_up.shape), BF16),
            pltpu.VMEM((2, *w_down.shape), BF16),
            pltpu.VMEM((2, 2, 8, LANES), BF16),
            pltpu.VMEM((2, 2, ROWS, 8, LANES), BF16),
            pltpu.VMEM((ROWS * 16, LANES), F32),
            pltpu.VMEM((2, 2, TOK // 2, wide), BF16),
            pltpu.VMEM((2, TOK // 2, wide), BF16),
            pltpu.VMEM((2, NZ, 16, width), BF16),
            pltpu.VMEM((2, NZ, 16, width), BF16),
            pltpu.VMEM((2, 2, NZ, 16, half_width), BF16),
            pltpu.VMEM((2, TOK // 2, width), BF16),
            pltpu.VMEM((ROWS * 16, LANES), F32),
            pltpu.VMEM((2, ROWS, 16, LANES), BF16),
            pltpu.VMEM((2, ROWS - 1, 16, LANES), BF16),
            pltpu.VMEM((2, 2, 8, LANES), F32),
            pltpu.VMEM((2, 8, LANES), F32),
            pltpu.VMEM((2, 8, LANES), F32),
            pltpu.VMEM((2, 8, LANES), F32),
            pltpu.VMEM((8, LANES), F32),
            pltpu.VMEM((16, LANES), BF16),
            pltpu.VMEM((ROWS, 16, LANES), BF16),
            pltpu.VMEM((2, TOK // 2, wide), BF16),
            pltpu.VMEM((2, TOK // 2, wide), BF16),
            pltpu.VMEM((NZ, 16, half_width), BF16),
            pltpu.VMEM((NZ, 16, half_width), BF16),
            pltpu.VMEM((2, NZ, 16, width), BF16),
            pltpu.VMEM((2, TOK // 2, width), F32),
            pltpu.VMEM((2, NZ, 16, half_width), BF16),
            pltpu.VMEM((2, 2, TOK // 2, width), BF16),
            pltpu.VMEM((2, ROWS, 8, LANES), BF16),
            pltpu.VMEM((2, ROWS, 8, LANES), BF16),
            *(pltpu.VMEM(a.shape, BF16) for a in outs),
            pltpu.SemaphoreType.DMA((NUM_SEMS,)),
            pltpu.SemaphoreType.DMA((NUM_SEMS,)),
            pltpu.SemaphoreType.DMA((7,)),
            pltpu.SemaphoreType.DMA((5,)),
        ],
        compiler_params=pltpu.CompilerParams(
            collective_id=0, has_side_effects=True, vmem_limit_bytes=VMEM_BYTES
        ),
        name="swiglu_step",
    )(target_rows, buckets, tokens, w_gate, w_up, w_down, target_table)
    return pl.pallas_call(
        write_out,
        out_shape=tuple(jax.ShapeDtypeStruct(a.shape, BF16) for a in outs),
        in_specs=[hbm] * 5,
        out_specs=(hbm,) * 5,
        scratch_shapes=[
            *(pltpu.VMEM(a.shape, BF16) for a in outs),
            pltpu.SemaphoreType.DMA((5 * PIECES,)),
            pltpu.SemaphoreType.DMA((5 * PIECES,)),
        ],
        compiler_params=pltpu.CompilerParams(vmem_limit_bytes=VMEM_BYTES),
        name="write_out",
    )(*results)


def solution(mesh):
    in_specs = (
        P("row", "col"),
        P("col", "row"),
        P("col", "row"),
        P("row", "col"),
        P(None, "col"),
        P("row"),
        P("row"),
    )
    out_specs = (
        P("row", "col"),
        P("row", "col"),
        P("col", "row"),
        P("col", "row"),
        P("row", "col"),
    )
    return jax.shard_map(
        on_device, mesh=mesh, in_specs=in_specs, out_specs=out_specs, check_vma=False
    )
```
